32 devices in a mesh: row: 4 (over y, x), col: 8 (over z, core).
Axes of the slice: x: 2, y: 2, z: 4, core: 2. Of those that a mesh axis runs over, the one named last changes fastest.
Arguments:
- tokens: bfloat16 [256, 16384], P('col', 'row'), may hold values from -6 to 6
- gate_weight: bfloat16 [16384, 28672], P('row', 'col'), may hold values from -0.078125 to 0.078125
- up_weight: bfloat16 [16384, 28672], P('row', 'col'), may hold values from -0.078125 to 0.078125
- down_weight: bfloat16 [28672, 16384], P('col', 'row'), may hold values from -0.0625 to 0.0625
- gate_mask: int32 [128, 224], P('row', 'col'), may hold values from 0 to 1, as said below
- up_mask: int32 [128, 224], P('row', 'col'), may hold values from 0 to 1, as said below
- down_mask: int32 [224, 128], P('col', 'row'), may hold values from 0 to 1, as said below
Outputs:
- mixed_output: bfloat16 [256, 16384], P('col', 'row')
The draws below stay inside these ranges and needn't reach their ends.
Inputs may be any that keep to these rules, and one draw needn't show every extreme that they name: `gate_mask`: 1 keeps a 128 x 128 block of the weight, 0 drops it. `up_mask`: 1 keeps a 128 x 128 block of the weight, 0 drops it. `down_mask`: 1 keeps a 128 x 128 block of the weight, 0 drops it.
All inputs are finite; a program needn't handle non-finite values.
Results may differ from the reference program's by a relative error of at most 0.0049.
Values may be sent and summed in bfloat16 or wider, within the bound.
No kernel may reach another device: no remote copies, remote signals or barrier semaphores. Data moves between devices by JAX's collectives and lax.ppermute only.
A program may use at most 256 MiB of HBM per device.

```python
import jax
import jax.numpy as jnp

D = 16384
FF = 28672
BLK = 128
TOKENS = 256


def block_pattern(key, block_rows, block_cols, hidden_dim):
    level_key, roll_key = jax.random.split(key)
    if hidden_dim == 1:
        level = jax.random.randint(level_key, (1, block_cols), 1, 6)
    else:
        level = jax.random.randint(level_key, (block_rows, 1), 1, 6)
    roll = jax.random.randint(roll_key, (block_rows, block_cols), 0, 10)
    return (roll < level).astype(jnp.int32)


def draw_gate_mask(key, part):
    return block_pattern(jax.random.fold_in(key, 11), D // BLK, FF // BLK, 1)


def draw_up_mask(key, part):
    return block_pattern(jax.random.fold_in(key, 12), D // BLK, FF // BLK, 1)


def draw_down_mask(key, part):
    return block_pattern(jax.random.fold_in(key, 13), FF // BLK, D // BLK, 0)


def shard_levels(rng, dims, cuts, low, high):
    level = 1.0
    for dim, shards_of in cuts:
        draws = jax.random.uniform(jax.random.fold_in(jax.random.fold_in(rng, 6), dim), (shards_of,), jnp.float32, low / len(cuts), high / len(cuts))
        level = level * jnp.repeat(jnp.exp(draws), dims[dim] // shards_of).reshape((-1,) + (1,) * (len(dims) - 1 - dim))
    return level


def bell_draw(key, dims, width, reach, cuts=(), kind=jnp.bfloat16):
    loudness = shard_levels(key, dims, cuts, -0.22, 0.18) if cuts else 1.0
    values = jax.random.normal(key, dims, jnp.float32) * width * loudness
    return jnp.minimum(jnp.maximum(values, -reach), reach).astype(kind)


def setup_inputs(seed: int = 0) -> dict:
    streams_of = jax.random.split(jax.random.key(seed), 8)
    tokens = bell_draw(streams_of[0], (TOKENS, D), 1.0, 6.0, ((0, 8), (1, 4)))
    gate_weight = bell_draw(streams_of[1], (D, FF), (3 * D // 10) ** -0.5, 0.078125, ((0, 4), (1, 8)))
    up_weight = bell_draw(streams_of[2], (D, FF), (3 * D // 10) ** -0.5, 0.078125, ((0, 4), (1, 8)))
    down_weight = bell_draw(streams_of[3], (FF, D), (3 * FF // 10) ** -0.5, 0.0625, ((0, 8), (1, 4)))
    gate_mask = draw_gate_mask(jax.random.fold_in(streams_of[7], 71), 0)
    up_mask = draw_up_mask(jax.random.fold_in(streams_of[7], 71), 0)
    down_mask = draw_down_mask(jax.random.fold_in(streams_of[7], 71), 0)
    return dict(tokens=tokens, gate_weight=gate_weight, up_weight=up_weight, down_weight=down_weight, gate_mask=gate_mask, up_mask=up_mask, down_mask=down_mask)


def apply_blocks(weight, mask):
    block_rows, block_cols = mask.shape
    shaped = weight.reshape(block_rows, weight.shape[0] // block_rows, block_cols, weight.shape[1] // block_cols)
    kept = shaped * mask.astype(weight.dtype)[:, None, :, None]
    return kept.reshape(weight.shape)


def reference(tokens, gate_weight, up_weight, down_weight, gate_mask, up_mask, down_mask):
    gate = jnp.dot(tokens, apply_blocks(gate_weight, gate_mask), preferred_element_type=jnp.float32)
    upward = jnp.dot(tokens, apply_blocks(up_weight, up_mask), preferred_element_type=jnp.float32)
    hidden = (jax.nn.silu(gate) * upward).astype(jnp.bfloat16)
    result = jnp.dot(hidden, apply_blocks(down_weight, down_mask), preferred_element_type=jnp.float32)
    return result.astype(jnp.bfloat16)
```

```python
import functools

import jax
import jax.numpy as jnp
from jax import lax
from jax.experimental import pallas as pl
from jax.experimental.pallas import tpu as pltpu
from jax.sharding import PartitionSpec as P

BF16 = jnp.bfloat16
F32 = jnp.float32
MIB = 1 << 20


def apply_blocks(weight, mask):
    block_rows, block_cols = mask.shape
    shaped = weight.reshape(
        block_rows, weight.shape[0] // block_rows, block_cols, weight.shape[1] // block_cols
    )
    kept = shaped * mask.astype(weight.dtype)[:, None, :, None]
    return kept.reshape(weight.shape)


def plain(tokens, gate_weight, up_weight, down_weight, gate_mask, up_mask, down_mask):
    rows = lax.all_gather(tokens, "col", axis=0, tiled=True)
    gate = jnp.dot(rows, apply_blocks(gate_weight, gate_mask), preferred_element_type=F32)
    up = jnp.dot(rows, apply_blocks(up_weight, up_mask), preferred_element_type=F32)
    gate, up = lax.psum(jnp.stack([gate, up]), "row")
    hidden = (jax.nn.silu(gate) * up).astype(BF16)
    part = jnp.dot(hidden, apply_blocks(down_weight, down_mask), preferred_element_type=F32)
    return lax.psum_scatter(part, "col", scatter_dimension=0, tiled=True).astype(BF16)


VMEM_SPEC = pl.BlockSpec(memory_space=pltpu.VMEM)
HBM_SPEC = pl.BlockSpec(memory_space=pltpu.HBM)
ANY_SPEC = pl.BlockSpec(memory_space=pl.ANY)


def in_hbm(value):
    return pltpu.with_memory_space_constraint(value, pltpu.HBM)


def in_vmem(value):
    return pltpu.with_memory_space_constraint(value, pltpu.VMEM)


def factor(mask, i, j):
    return mask[i, j].astype(F32).astype(BF16)


def loop(count, step, unroll=1):
    def body(i, carry):
        step(i)
        return carry

    lax.fori_loop(0, count, body, 0, unroll=unroll)


def cost(flops, count):
    return pl.CostEstimate(flops=flops, bytes_accessed=count, transcendentals=0)


def nothing(*refs):
    del refs


def tie(value, *deps):
    return pl.pallas_call(
        nothing,
        in_specs=[ANY_SPEC] * (1 + len(deps)),
        out_specs=ANY_SPEC,
        out_shape=jax.ShapeDtypeStruct(value.shape, value.dtype),
        input_output_aliases={0: 0},
        compiler_params=pltpu.CompilerParams(vmem_limit_bytes=MIB),
        name="tie",
    )(value, *deps)


def quarter_of(name):
    row, col = lax.axis_index("row"), lax.axis_index("col")
    step1 = 1 + lax.rem(col, 2)
    flip = {"own": 0, "second": 3 - step1, "first": step1, "last": 3}[name]
    return row ^ flip


class Pairs:
    def __init__(self, quarter, masks, weights, buf, held_masks, sem, mask_sem):
        self.quarter, self.masks, self.weights = quarter, masks, weights
        self.buf, self.held_masks, self.sem, self.mask_sem = buf, held_masks, sem, mask_sem
        self.tiles, self.depth, self.wide = buf.shape
        self.blk = self.wide // 2

    def mask_copies(self):
        return [
            pltpu.make_async_copy(m, h, self.mask_sem.at[t])
            for t, (m, h) in enumerate(zip(self.masks, self.held_masks))
        ]

    def copies(self, tile):
        column = pl.multiple_of((self.quarter * self.tiles + tile) * self.blk, self.blk)
        return [
            pltpu.make_async_copy(
                w.at[:, pl.ds(column, self.blk)],
                self.buf.at[tile, :, pl.ds(t * self.blk, self.blk)],
                self.sem.at[tile, t],
            )
            for t, w in enumerate(self.weights)
        ]

    def start(self):
        for copy in self.mask_copies():
            copy.start()

        def step(tile):
            for copy in self.copies(tile):
                copy.start()

        loop(self.tiles, step)
        for copy in self.mask_copies():
            copy.wait()

    def wait(self, tile):
        for copy in self.copies(tile):
            copy.wait()

    def masked(self, tile):
        blk = self.blk
        column = self.quarter * self.tiles + tile
        return [
            [
                self.buf[tile, a * blk : (a + 1) * blk, t * blk : (t + 1) * blk] * factor(m, a, column)
                for t, m in enumerate(self.held_masks)
            ]
            for a in range(self.depth // blk)
        ]


def pairs_scratch(mask, tiles):
    return [
        pltpu.SMEM(mask.shape, mask.dtype),
        pltpu.SMEM(mask.shape, mask.dtype),
        pltpu.SemaphoreType.DMA((tiles, 2)),
        pltpu.SemaphoreType.DMA((2,)),
    ]


def put_pair(out, tile, value):
    blk = value.shape[1] // 2
    half = out.shape[1] // 2
    for t in range(2):
        column = pl.multiple_of(t * half + tile * blk, blk)
        out[:, pl.ds(column, blk)] = value[:, t * blk : (t + 1) * blk].astype(out.dtype)


def get_pair(got, tile, blk):
    half = got[0].shape[1] // 2
    columns = [pl.ds(pl.multiple_of(t * half + tile * blk, blk), blk) for t in range(2)]
    return jnp.concatenate(
        [jnp.concatenate([part[:, at].astype(F32) for at in columns], axis=1) for part in got], axis=0
    )


def load_pairs_kernel(name, *refs):
    buf, *held_masks, sem, mask_sem = refs[-5:]
    pairs = Pairs(quarter_of(name), refs[:2], refs[2:4], buf, held_masks, sem, mask_sem)
    blk = pairs.blk
    pairs.start()

    def keep(tile):
        pairs.wait(tile)
        for a, blocks in enumerate(pairs.masked(tile)):
            for t, value in enumerate(blocks):
                buf[tile, a * blk : (a + 1) * blk, t * blk : (t + 1) * blk] = value

    loop(pairs.tiles, keep)


def load_pairs(name, masks, weights, deps=()):
    depth, width = weights[0].shape
    blk = width // masks[0].shape[1]
    tiles = masks[0].shape[1] // 4
    return pl.pallas_call(
        functools.partial(load_pairs_kernel, name),
        in_specs=[HBM_SPEC] * 4 + [ANY_SPEC] * len(deps),
        out_specs=VMEM_SPEC,
        out_shape=pltpu.VMEM((tiles, depth, 2 * blk), BF16),
        scratch_shapes=pairs_scratch(masks[0], tiles),
        compiler_params=pltpu.CompilerParams(vmem_limit_bytes=4 * MIB),
        cost_estimate=cost(0, 2 * 2 * depth * width // 4),
        name="load_" + name,
    )(*[in_hbm(v) for v in (*masks, *weights)], *deps)


def held_pairs_kernel(count, added, *refs):
    x, buf, got, out = refs[:count], refs[count], refs[count + 1 : count + 1 + added], refs[-1]

    def step(tile):
        rows = jnp.concatenate([part[...] for part in x], axis=0)
        value = jnp.dot(rows, buf[tile], preferred_element_type=F32)
        if added:
            value = value + get_pair(got, tile, buf.shape[2] // 2)
        put_pair(out, tile, value)

    loop(buf.shape[0], step, unroll=buf.shape[0])


def held_pairs(x, buf, added=(), deps=()):
    tiles, depth, wide = buf.shape
    rows = sum(part.shape[0] for part in x)
    return pl.pallas_call(
        functools.partial(held_pairs_kernel, len(x), len(added)),
        in_specs=[VMEM_SPEC] * (len(x) + 1 + len(added)) + [ANY_SPEC] * len(deps),
        out_specs=VMEM_SPEC,
        out_shape=jax.ShapeDtypeStruct((rows, tiles * wide), BF16),
        compiler_params=pltpu.CompilerParams(vmem_limit_bytes=4 * MIB),
        cost_estimate=cost(2 * rows * depth * tiles * wide, 2 * tiles * depth * wide // 2),
        name="held_pairs",
    )(*[in_vmem(part) for part in x], in_vmem(buf), *[in_vmem(part) for part in added], *deps)


def stream_pairs_kernel(name, count, rows, *refs):
    x, outs = refs[4 : 4 + count], refs[-5 - len(rows) : -5]
    buf, *held_masks, sem, mask_sem = refs[-5:]
    pairs = Pairs(quarter_of(name), refs[:2], refs[2:4], buf, held_masks, sem, mask_sem)
    pairs.start()

    def step(tile):
        pairs.wait(tile)
        w = jnp.concatenate([jnp.concatenate(row, axis=1) for row in pairs.masked(tile)], axis=0)
        value = jnp.dot(jnp.concatenate([part[...] for part in x], axis=0), w, preferred_element_type=F32)
        first = 0
        for size, out in zip(rows, outs):
            put_pair(out, tile, value[first : first + size])
            first += size

    loop(pairs.tiles, step)


def stream_pairs(name, masks, weights, groups, deps=()):
    depth, width = weights[0].shape
    blk = width // masks[0].shape[1]
    tiles = masks[0].shape[1] // 4
    x = [part for group in groups for part in group]
    rows = [sum(part.shape[0] for part in group) for group in groups]
    return pl.pallas_call(
        functools.partial(stream_pairs_kernel, name, len(x), rows),
        in_specs=[HBM_SPEC] * 4 + [VMEM_SPEC] * len(x) + [ANY_SPEC] * len(deps),
        out_specs=[VMEM_SPEC] * len(rows),
        out_shape=[jax.ShapeDtypeStruct((size, width // 2), F32) for size in rows],
        scratch_shapes=[pltpu.VMEM((tiles, depth, 2 * blk), BF16)] + pairs_scratch(masks[0], tiles),
        compiler_params=pltpu.CompilerParams(vmem_limit_bytes=22 * MIB),
        cost_estimate=cost(2 * sum(rows) * depth * width // 2, 2 * 2 * depth * width // 4),
        name="stream_" + name,
    )(*[in_hbm(v) for v in (*masks, *weights)], *[in_vmem(part) for part in x], *deps)


def load_down_kernel(names, mask_hbm, down_hbm, *refs):
    count = len(names)
    bufs, (mask, sem, mask_sem) = refs[-3 - count : -3], refs[-3:]
    panels, depth, width = bufs[0].shape
    cols = mask.shape[1]
    blk = width // cols
    first = [quarter_of(name) * panels for name in names]
    mask_copy = pltpu.make_async_copy(mask_hbm, mask, mask_sem)

    def copy(k, p):
        rows = pl.ds(pl.multiple_of((first[k] + p) * depth, depth), depth)
        return pltpu.make_async_copy(down_hbm.at[rows], bufs[k].at[p], sem.at[k, p])

    mask_copy.start()
    for k in range(count):
        loop(panels, lambda p, k=k: copy(k, p).start())
    mask_copy.wait()
    for k in range(count):

        def keep(p, k=k):
            copy(k, p).wait()
            for j in range(cols):
                at = slice(j * blk, (j + 1) * blk)
                bufs[k][p, :, at] = bufs[k][p, :, at] * factor(mask, first[k] + p, j)

        loop(panels, keep)


def load_down(names, mask, down, deps=()):
    count = len(names)
    panels = mask.shape[0] // 4
    depth, width = down.shape
    return pl.pallas_call(
        functools.partial(load_down_kernel, names),
        in_specs=[HBM_SPEC] * 2 + [ANY_SPEC] * len(deps),
        out_specs=[VMEM_SPEC] * count,
        out_shape=[pltpu.VMEM((panels, depth // mask.shape[0], width), BF16)] * count,
        scratch_shapes=[
            pltpu.SMEM(mask.shape, mask.dtype),
            pltpu.SemaphoreType.DMA((count, panels)),
            pltpu.SemaphoreType.DMA,
        ],
        compiler_params=pltpu.CompilerParams(vmem_limit_bytes=4 * MIB),
        cost_estimate=cost(0, 2 * depth * width * count // 4),
        name="load_down",
    )(in_hbm(mask), in_hbm(down), *deps)


def held_down_kernel(tile, count, *refs):
    hidden, bufs, (mine, other, rows) = refs[:count], refs[count : 2 * count], refs[-3:]
    panels, blk, width = bufs[0].shape
    half = mine.shape[0]
    for k, part in enumerate(hidden):
        rows[:, k * panels * blk : (k + 1) * panels * blk] = part[...]

    def step(n):
        at = pl.ds(pl.multiple_of(n * tile, tile), tile)
        w = jnp.concatenate([buf[:, :, at].reshape(panels * blk, tile) for buf in bufs], axis=0)
        total = jnp.dot(rows[...], w, preferred_element_type=F32)
        mine[:, at] = total[:half]
        other[:, at] = total[half:].astype(other.dtype)

    loop(width // tile, step, unroll=2)


def held_down(hidden, bufs, dtype, tile=256, deps=()):
    panels, blk, width = bufs[0].shape
    rows = hidden[0].shape[0]
    depth = panels * blk * len(hidden)
    return pl.pallas_call(
        functools.partial(held_down_kernel, tile, len(hidden)),
        in_specs=[VMEM_SPEC] * (2 * len(hidden)) + [ANY_SPEC] * len(deps),
        out_specs=[VMEM_SPEC] * 2,
        out_shape=[
            jax.ShapeDtypeStruct((rows // 2, width), F32),
            jax.ShapeDtypeStruct((rows // 2, width), dtype),
        ],
        scratch_shapes=[pltpu.VMEM((rows, depth), BF16)],
        compiler_params=pltpu.CompilerParams(vmem_limit_bytes=4 * MIB),
        cost_estimate=cost(2 * rows * depth * width, 2 * depth * width // 2),
        name="held_down",
    )(*[in_vmem(h) for h in hidden], *[in_vmem(b) for b in bufs], *deps)


def gated_kernel(first, own, got_first, got_second, *refs):
    out = refs[-1]
    rows, width = out.shape
    gate, up = [
        own[:, at] + got_first[:, at].astype(F32) + got_second[first : first + rows, at].astype(F32)
        for at in (slice(0, width), slice(width, 2 * width))
    ]
    out[...] = (jax.nn.silu(gate) * up).astype(out.dtype)


def gated(own, got_first, got_second, first, deps=()):
    rows, width = own.shape
    return pl.pallas_call(
        functools.partial(gated_kernel, first),
        in_specs=[VMEM_SPEC] * 3 + [ANY_SPEC] * len(deps),
        out_specs=VMEM_SPEC,
        out_shape=jax.ShapeDtypeStruct((rows, width // 2), BF16),
        compiler_params=pltpu.CompilerParams(vmem_limit_bytes=8 * MIB),
        cost_estimate=cost(0, 8 * rows * width),
        name="gated",
    )(in_vmem(own), in_vmem(got_first), in_vmem(got_second), *deps)


class Exchange:
    def __init__(self, rows, cols):
        self.rows, self.cols = rows, cols

    def swap(self, value, row_bits, col_bits):
        pairs = []
        for r in range(self.rows):
            for c in range(self.cols):
                pairs.append((r * self.cols + c, (r ^ row_bits(c)) * self.cols + (c ^ col_bits)))
        return lax.ppermute(value, ("row", "col"), pairs)

    def core(self, value):
        return self.swap(value, lambda c: 0, 1)

    def near(self, value):
        return self.swap(value, lambda c: 0, 2)

    def far(self, value):
        return self.swap(value, lambda c: 0, 4)

    def first(self, value):
        return self.swap(value, lambda c: 1 + (c & 1), 0)

    def second(self, value):
        return self.swap(value, lambda c: 2 - (c & 1), 0)


def paired(tokens, gate_weight, up_weight, down_weight, gate_mask, up_mask, down_mask, swap):
    weights = (gate_weight, up_weight)
    masks = (gate_mask, up_mask)
    width = gate_weight.shape[1] // 4
    blk = tokens.shape[0]

    near = swap.near(tokens)
    far = swap.far(tokens)
    core = swap.core(tokens)
    w_last = load_pairs("last", masks, weights)
    w_first = load_pairs("first", masks, weights, deps=(w_last,))
    near = tie(near, w_first)
    far = tie(far, w_first)
    far_near = swap.near(far)
    close = (tokens, near, core, swap.core(near))
    close_last = held_pairs(close, w_last)
    got_close_last = swap.first(close_last)
    w_second = load_pairs("second", masks, weights, deps=(close_last,))
    far_near = tie(far_near, w_second)
    distant = (far, far_near, swap.core(far), swap.core(far_near))
    distant_last = held_pairs(distant, w_last, deps=(got_close_last,))
    got_distant_last = swap.first(distant_last)
    close_first = held_pairs(close, w_first, deps=(distant_last,))
    got_close_first = swap.first(close_first)
    distant_first = held_pairs(distant, w_first, deps=(close_first,))
    got_distant_first = swap.first(distant_first)
    second = held_pairs(
        distant + close, w_second, added=(got_distant_last, got_close_last), deps=(distant_first,)
    )
    second = tie(second, got_close_first)
    got_second = swap.second(second)
    distant_own, close_own = stream_pairs("own", masks, weights, (distant, close), deps=(second,))
    w_down = load_down(("own",), down_mask, down_weight, deps=(distant_own, got_distant_first))

    distant_hidden = gated(distant_own, got_distant_first, got_second, 0, deps=w_down)
    close_hidden = gated(close_own, got_close_first, got_second, 4 * blk, deps=(distant_hidden,))
    w_down += load_down(("second", "first"), down_mask, down_weight, deps=(close_hidden,))

    def gathered(hidden):
        second, first = swap.second(hidden), swap.first(hidden)
        second = tie(second, w_down[1])
        return [hidden, second, first, swap.first(second)]

    distant_hidden = gathered(distant_hidden)
    close_hidden = gathered(close_hidden)
    w_down += load_down(("last",), down_mask, down_weight, deps=(distant_hidden[1],))

    mine, other = held_down(distant_hidden, w_down, F32, deps=close_hidden)
    mine = mine + swap.core(other)
    near_sum = mine[blk:].astype(BF16)
    got_near = swap.near(near_sum)
    got_far = swap.far((mine[:blk] + got_near).astype(BF16))
    mine, other = held_down(close_hidden, w_down, F32, deps=(near_sum,))
    mine = mine + swap.core(other)
    got_near = swap.near(mine[blk:].astype(BF16))
    return (mine[:blk] + got_near + got_far).astype(BF16)


def solution(mesh):
    rows, cols = mesh.shape["row"], mesh.shape["col"]
    body = plain
    if (rows, cols) == (4, 8):
        body = functools.partial(paired, swap=Exchange(rows, cols))
    return jax.shard_map(
        body,
        mesh=mesh,
        in_specs=(
            P("col", "row"),
            P("row", "col"),
            P("row", "col"),
            P("col", "row"),
            P("row", "col"),
            P("row", "col"),
            P("col", "row"),
        ),
        out_specs=P("col", "row"),
        check_vma=False,
    )
```

```python
import functools

import jax
import jax.numpy as jnp
from jax import lax
from jax.experimental import pallas as pl
from jax.experimental.pallas import tpu as pltpu
from jax.sharding import PartitionSpec as P

BF16 = jnp.bfloat16
F32 = jnp.float32
MIB = 1 << 20


def apply_blocks(weight, mask):
    block_rows, block_cols = mask.shape
    shaped = weight.reshape(
        block_rows, weight.shape[0] // block_rows, block_cols, weight.shape[1] // block_cols
    )
    kept = shaped * mask.astype(weight.dtype)[:, None, :, None]
    return kept.reshape(weight.shape)


def plain(tokens, gate_weight, up_weight, down_weight, gate_mask, up_mask, down_mask):
    rows = lax.all_gather(tokens, "col", axis=0, tiled=True)
    gate = jnp.dot(rows, apply_blocks(gate_weight, gate_mask), preferred_element_type=F32)
    up = jnp.dot(rows, apply_blocks(up_weight, up_mask), preferred_element_type=F32)
    gate, up = lax.psum(jnp.stack([gate, up]), "row")
    hidden = (jax.nn.silu(gate) * up).astype(BF16)
    part = jnp.dot(hidden, apply_blocks(down_weight, down_mask), preferred_element_type=F32)
    return lax.psum_scatter(part, "col", scatter_dimension=0, tiled=True).astype(BF16)


VMEM_SPEC = pl.BlockSpec(memory_space=pltpu.VMEM)
HBM_SPEC = pl.BlockSpec(memory_space=pltpu.HBM)
ANY_SPEC = pl.BlockSpec(memory_space=pl.ANY)


def in_hbm(value):
    return pltpu.with_memory_space_constraint(value, pltpu.HBM)


def in_vmem(value):
    return pltpu.with_memory_space_constraint(value, pltpu.VMEM)


def factor(mask, i, j):
    return mask[i, j].astype(F32).astype(BF16)


def loop(count, step, unroll=1):
    def body(i, carry):
        step(i)
        return carry

    lax.fori_loop(0, count, body, 0, unroll=unroll)


def cost(flops, count):
    return pl.CostEstimate(flops=flops, bytes_accessed=count, transcendentals=0)


def nothing(*refs):
    del refs


def tie(value, *deps):
    return pl.pallas_call(
        nothing,
        in_specs=[ANY_SPEC] * (1 + len(deps)),
        out_specs=ANY_SPEC,
        out_shape=jax.ShapeDtypeStruct(value.shape, value.dtype),
        input_output_aliases={0: 0},
        compiler_params=pltpu.CompilerParams(vmem_limit_bytes=MIB),
        name="tie",
    )(value, *deps)


def quarter_of(name):
    row, col = lax.axis_index("row"), lax.axis_index("col")
    step1 = 1 + lax.rem(col, 2)
    flip = {"own": 0, "second": 3 - step1, "first": step1, "last": 3}[name]
    return row ^ flip


class Pairs:
    def __init__(self, quarter, masks, weights, buf, held_masks, sem, mask_sem):
        self.quarter, self.masks, self.weights = quarter, masks, weights
        self.buf, self.held_masks, self.sem, self.mask_sem = buf, held_masks, sem, mask_sem
        self.tiles, self.depth, self.wide = buf.shape
        self.blk = self.wide // 2

    def mask_copies(self):
        return [
            pltpu.make_async_copy(m, h, self.mask_sem.at[t])
            for t, (m, h) in enumerate(zip(self.masks, self.held_masks))
        ]

    def copies(self, tile):
        column = pl.multiple_of((self.quarter * self.tiles + tile) * self.blk, self.blk)
        return [
            pltpu.make_async_copy(
                w.at[:, pl.ds(column, self.blk)],
                self.buf.at[tile, :, pl.ds(t * self.blk, self.blk)],
                self.sem.at[tile, t],
            )
            for t, w in enumerate(self.weights)
        ]

    def start(self):
        for copy in self.mask_copies():
            copy.start()

        def step(tile):
            for copy in self.copies(tile):
                copy.start()

        loop(self.tiles, step)
        for copy in self.mask_copies():
            copy.wait()

    def wait(self, tile):
        for copy in self.copies(tile):
            copy.wait()

    def masked(self, tile):
        blk = self.blk
        column = self.quarter * self.tiles + tile
        return [
            [
                self.buf[tile, a * blk : (a + 1) * blk, t * blk : (t + 1) * blk] * factor(m, a, column)
                for t, m in enumerate(self.held_masks)
            ]
            for a in range(self.depth // blk)
        ]


def pairs_scratch(mask, tiles):
    return [
        pltpu.SMEM(mask.shape, mask.dtype),
        pltpu.SMEM(mask.shape, mask.dtype),
        pltpu.SemaphoreType.DMA((tiles, 2)),
        pltpu.SemaphoreType.DMA((2,)),
    ]


def put_pair(out, tile, value):
    blk = value.shape[1] // 2
    half = out.shape[1] // 2
    for t in range(2):
        column = pl.multiple_of(t * half + tile * blk, blk)
        out[:, pl.ds(column, blk)] = value[:, t * blk : (t + 1) * blk].astype(out.dtype)


def load_pairs_kernel(name, *refs):
    buf, *held_masks, sem, mask_sem = refs[-5:]
    pairs = Pairs(quarter_of(name), refs[:2], refs[2:4], buf, held_masks, sem, mask_sem)
    blk = pairs.blk
    pairs.start()

    def keep(tile):
        pairs.wait(tile)
        for a, blocks in enumerate(pairs.masked(tile)):
            for t, value in enumerate(blocks):
                buf[tile, a * blk : (a + 1) * blk, t * blk : (t + 1) * blk] = value

    loop(pairs.tiles, keep)


def load_pairs(name, masks, weights, deps=()):
    depth, width = weights[0].shape
    blk = width // masks[0].shape[1]
    tiles = masks[0].shape[1] // 4
    return pl.pallas_call(
        functools.partial(load_pairs_kernel, name),
        in_specs=[HBM_SPEC] * 4 + [ANY_SPEC] * len(deps),
        out_specs=VMEM_SPEC,
        out_shape=pltpu.VMEM((tiles, depth, 2 * blk), BF16),
        scratch_shapes=pairs_scratch(masks[0], tiles),
        compiler_params=pltpu.CompilerParams(vmem_limit_bytes=4 * MIB),
        cost_estimate=cost(0, 2 * 2 * depth * width // 4),
        name="load_" + name,
    )(*[in_hbm(v) for v in (*masks, *weights)], *deps)


def held_pairs_kernel(count, *refs):
    x, buf, out = refs[:count], refs[count], refs[-1]

    def step(tile):
        rows = jnp.concatenate([part[...] for part in x], axis=0)
        put_pair(out, tile, jnp.dot(rows, buf[tile], preferred_element_type=F32))

    loop(buf.shape[0], step, unroll=buf.shape[0])


def held_pairs(x, buf, deps=()):
    tiles, depth, wide = buf.shape
    rows = sum(part.shape[0] for part in x)
    return pl.pallas_call(
        functools.partial(held_pairs_kernel, len(x)),
        in_specs=[VMEM_SPEC] * (len(x) + 1) + [ANY_SPEC] * len(deps),
        out_specs=VMEM_SPEC,
        out_shape=jax.ShapeDtypeStruct((rows, tiles * wide), BF16),
        compiler_params=pltpu.CompilerParams(vmem_limit_bytes=4 * MIB),
        cost_estimate=cost(2 * rows * depth * tiles * wide, 2 * tiles * depth * wide // 2),
        name="held_pairs",
    )(*[in_vmem(part) for part in x], in_vmem(buf), *deps)


def stream_pairs_kernel(name, count, rows, *refs):
    x, outs = refs[4 : 4 + count], refs[-5 - len(rows) : -5]
    buf, *held_masks, sem, mask_sem = refs[-5:]
    pairs = Pairs(quarter_of(name), refs[:2], refs[2:4], buf, held_masks, sem, mask_sem)
    pairs.start()

    def step(tile):
        pairs.wait(tile)
        w = jnp.concatenate([jnp.concatenate(row, axis=1) for row in pairs.masked(tile)], axis=0)
        value = jnp.dot(jnp.concatenate([part[...] for part in x], axis=0), w, preferred_element_type=F32)
        first = 0
        for size, out in zip(rows, outs):
            put_pair(out, tile, value[first : first + size])
            first += size

    loop(pairs.tiles, step)


def stream_pairs(name, masks, weights, groups, deps=()):
    depth, width = weights[0].shape
    blk = width // masks[0].shape[1]
    tiles = masks[0].shape[1] // 4
    x = [part for group in groups for part in group]
    rows = [sum(part.shape[0] for part in group) for group in groups]
    return pl.pallas_call(
        functools.partial(stream_pairs_kernel, name, len(x), rows),
        in_specs=[HBM_SPEC] * 4 + [VMEM_SPEC] * len(x) + [ANY_SPEC] * len(deps),
        out_specs=[VMEM_SPEC] * len(rows),
        out_shape=[jax.ShapeDtypeStruct((size, width // 2), F32) for size in rows],
        scratch_shapes=[pltpu.VMEM((tiles, depth, 2 * blk), BF16)] + pairs_scratch(masks[0], tiles),
        compiler_params=pltpu.CompilerParams(vmem_limit_bytes=22 * MIB),
        cost_estimate=cost(2 * sum(rows) * depth * width // 2, 2 * 2 * depth * width // 4),
        name="stream_" + name,
    )(*[in_hbm(v) for v in (*masks, *weights)], *[in_vmem(part) for part in x], *deps)


def load_down_kernel(names, mask_hbm, down_hbm, *refs):
    count = len(names)
    bufs, (mask, sem, mask_sem) = refs[-3 - count : -3], refs[-3:]
    panels, depth, width = bufs[0].shape
    cols = mask.shape[1]
    blk = width // cols
    first = [quarter_of(name) * panels for name in names]
    mask_copy = pltpu.make_async_copy(mask_hbm, mask, mask_sem)

    def copy(k, p):
        rows = pl.ds(pl.multiple_of((first[k] + p) * depth, depth), depth)
        return pltpu.make_async_copy(down_hbm.at[rows], bufs[k].at[p], sem.at[k, p])

    mask_copy.start()
    for k in range(count):
        loop(panels, lambda p, k=k: copy(k, p).start())
    mask_copy.wait()
    for k in range(count):

        def keep(p, k=k):
            copy(k, p).wait()
            for j in range(cols):
                at = slice(j * blk, (j + 1) * blk)
                bufs[k][p, :, at] = bufs[k][p, :, at] * factor(mask, first[k] + p, j)

        loop(panels, keep)


def load_down(names, mask, down, deps=()):
    count = len(names)
    panels = mask.shape[0] // 4
    depth, width = down.shape
    return pl.pallas_call(
        functools.partial(load_down_kernel, names),
        in_specs=[HBM_SPEC] * 2 + [ANY_SPEC] * len(deps),
        out_specs=[VMEM_SPEC] * count,
        out_shape=[pltpu.VMEM((panels, depth // mask.shape[0], width), BF16)] * count,
        scratch_shapes=[
            pltpu.SMEM(mask.shape, mask.dtype),
            pltpu.SemaphoreType.DMA((count, panels)),
            pltpu.SemaphoreType.DMA,
        ],
        compiler_params=pltpu.CompilerParams(vmem_limit_bytes=4 * MIB),
        cost_estimate=cost(0, 2 * depth * width * count // 4),
        name="load_down",
    )(in_hbm(mask), in_hbm(down), *deps)


def down_kernel(count, adds, blocks, tile, *refs):
    hidden, bufs, total = refs[:count], refs[count : 2 * count], refs[2 * count]
    outs, rows = refs[-1 - blocks : -1], refs[-1]
    panels, blk, width = bufs[0].shape
    depth = panels * blk
    for k, part in enumerate(hidden):
        rows[:, k * depth : (k + 1) * depth] = part[...]

    def step(n):
        at = pl.ds(pl.multiple_of(n * tile, tile), tile)
        w = jnp.concatenate([buf[:, :, at].reshape(depth, tile) for buf in bufs], axis=0)
        value = jnp.dot(rows[...], w, preferred_element_type=F32)
        if adds:
            value = value + total[:, at]
        size = value.shape[0] // blocks
        for k, out in enumerate(outs):
            out[:, at] = value[k * size : (k + 1) * size]

    loop(width // tile, step, unroll=2)


def down(hidden, bufs, total=(), blocks=1, tile=512, deps=()):
    panels, blk, width = bufs[0].shape
    rows, depth, count = hidden[0].shape[0], len(hidden) * panels * blk, len(hidden)
    return pl.pallas_call(
        functools.partial(down_kernel, count, len(total), blocks, tile),
        in_specs=[VMEM_SPEC] * (2 * count + len(total)) + [ANY_SPEC] * len(deps),
        out_specs=[VMEM_SPEC] * blocks,
        out_shape=[jax.ShapeDtypeStruct((rows // blocks, width), F32)] * blocks,
        scratch_shapes=[pltpu.VMEM((rows, depth), BF16)],
        compiler_params=pltpu.CompilerParams(vmem_limit_bytes=4 * MIB),
        cost_estimate=cost(2 * rows * depth * width, 2 * depth * width),
        name="down",
    )(*[in_vmem(v) for v in (*hidden, *bufs, *total)], *deps)


def added_kernel(count, *refs):
    base, parts, out = refs[0], refs[1 : 1 + count], refs[-1]
    first = 0
    for part in parts:
        at = slice(first, first + part.shape[0])
        out[at] = (base[at] + part[...].astype(F32)).astype(out.dtype)
        first += part.shape[0]


def added(base, parts, deps=()):
    return pl.pallas_call(
        functools.partial(added_kernel, len(parts)),
        in_specs=[VMEM_SPEC] * (1 + len(parts)) + [ANY_SPEC] * len(deps),
        out_specs=VMEM_SPEC,
        out_shape=jax.ShapeDtypeStruct(base.shape, BF16),
        compiler_params=pltpu.CompilerParams(vmem_limit_bytes=4 * MIB),
        cost_estimate=cost(0, 8 * base.size),
        name="added",
    )(*[in_vmem(v) for v in (base, *parts)], *deps)


def gated_kernel(first, own, got_first, got_second, *refs):
    out = refs[-1]
    rows, width = out.shape
    gate, up = [
        own[:, at] + got_first[:, at].astype(F32) + got_second[first : first + rows, at].astype(F32)
        for at in (slice(0, width), slice(width, 2 * width))
    ]
    out[...] = (jax.nn.silu(gate) * up).astype(out.dtype)


def gated(own, got_first, got_second, first, deps=()):
    rows, width = own.shape
    return pl.pallas_call(
        functools.partial(gated_kernel, first),
        in_specs=[VMEM_SPEC] * 3 + [ANY_SPEC] * len(deps),
        out_specs=VMEM_SPEC,
        out_shape=jax.ShapeDtypeStruct((rows, width // 2), BF16),
        compiler_params=pltpu.CompilerParams(vmem_limit_bytes=8 * MIB),
        cost_estimate=cost(0, 8 * rows * width),
        name="gated",
    )(in_vmem(own), in_vmem(got_first), in_vmem(got_second), *deps)


class Exchange:
    def __init__(self, rows, cols):
        self.rows, self.cols = rows, cols

    def swap(self, value, row_bits, col_bits):
        pairs = []
        for r in range(self.rows):
            for c in range(self.cols):
                pairs.append((r * self.cols + c, (r ^ row_bits(c)) * self.cols + (c ^ col_bits)))
        return lax.ppermute(value, ("row", "col"), pairs)

    def core(self, value):
        return self.swap(value, lambda c: 0, 1)

    def near(self, value):
        return self.swap(value, lambda c: 0, 2)

    def far(self, value):
        return self.swap(value, lambda c: 0, 4)

    def diagonal(self, value):
        return self.swap(value, lambda c: 0, 6)

    def first(self, value):
        return self.swap(value, lambda c: 1 + (c & 1), 0)

    def second(self, value):
        return self.swap(value, lambda c: 2 - (c & 1), 0)


def paired(tokens, gate_weight, up_weight, down_weight, gate_mask, up_mask, down_mask, swap):
    weights = (gate_weight, up_weight)
    masks = (gate_mask, up_mask)
    width = gate_weight.shape[1] // 4
    blk = tokens.shape[0]

    near = swap.near(tokens)
    far = swap.far(tokens)
    core = swap.core(tokens)
    w_last = load_pairs("last", masks, weights)
    w_first = load_pairs("first", masks, weights, deps=(w_last,))
    near = tie(near, w_first)
    far = tie(far, w_first)
    far_near = swap.near(far)
    close = (tokens, near, core, swap.core(near))
    close_last = held_pairs(close, w_last)
    got_close_last = swap.first(close_last)
    close_first = held_pairs(close, w_first, deps=(close_last,))
    got_close_first = swap.first(close_first)
    far_near = tie(far_near, close_first)
    distant = (far, far_near, swap.core(far), swap.core(far_near))
    distant_last = tie(held_pairs(distant, w_last), got_close_last)
    got_distant_last = swap.first(distant_last)
    (second,) = stream_pairs(
        "second", masks, weights, (distant + close,), deps=(distant_last, close_first)
    )
    second = added(second, (got_distant_last, got_close_last), deps=(got_close_first,))
    got_second = swap.second(second)
    distant_first = held_pairs(distant, w_first, deps=(second,))
    got_distant_first = swap.first(distant_first)
    distant_own, close_own = stream_pairs("own", masks, weights, (distant, close), deps=(distant_first,))

    source = (down_mask, down_weight)
    down_own, down_second = load_down(("own", "second"), *source, deps=(distant_own,))
    distant = gated(distant_own, got_distant_first, got_second, 0, deps=(down_own,))
    close = gated(close_own, got_close_first, got_second, 4 * blk, deps=(distant,))
    second, first = swap.second(distant), swap.first(distant)
    down_first, down_last = load_down(("first", "last"), *source, deps=(close,))
    second = tie(second, down_last)
    last = swap.first(second)
    close = tie(close, second)
    close_second, close_first = swap.second(close), swap.first(close)
    total = down((distant, second, first), (down_own, down_second, down_first))
    mine, other = down((last,), (down_last,), total, blocks=2)
    other = tie(other, close_second, close_first)

    mine = mine + swap.core(other)
    total = down((close,), (down_own,), deps=(other,))
    close_second = tie(close_second, *total)
    close_last = swap.first(close_second)
    near_rows, far_rows = mine[blk:].astype(BF16), mine[:blk]
    got_near = swap.near(near_rows)
    total = down((close_second, close_first), (down_second, down_first), total, deps=(near_rows,))
    far_rows = (far_rows + got_near).astype(BF16)
    got_far = swap.far(far_rows)
    mine, other = down((close_last,), (down_last,), total, blocks=2)
    mine = mine + swap.core(tie(other, far_rows))
    return (mine[:blk] + swap.near(mine[blk:].astype(BF16)) + got_far).astype(BF16)


def solution(mesh):
    rows, cols = mesh.shape["row"], mesh.shape["col"]
    body = plain
    if (rows, cols) == (4, 8):
        body = functools.partial(paired, swap=Exchange(rows, cols))
    return jax.shard_map(
        body,
        mesh=mesh,
        in_specs=(
            P("col", "row"),
            P("row", "col"),
            P("row", "col"),
            P("col", "row"),
            P("row", "col"),
            P("row", "col"),
            P("col", "row"),
        ),
        out_specs=P("col", "row"),
        check_vma=False,
    )
```

```python
import functools

import jax
import jax.numpy as jnp
from jax import lax
from jax.experimental import pallas as pl
from jax.experimental.pallas import tpu as pltpu
from jax.sharding import PartitionSpec as P

BF16 = jnp.bfloat16
F32 = jnp.float32
MIB = 1 << 20


def apply_blocks(weight, mask):
    block_rows, block_cols = mask.shape
    shaped = weight.reshape(
        block_rows, weight.shape[0] // block_rows, block_cols, weight.shape[1] // block_cols
    )
    kept = shaped * mask.astype(weight.dtype)[:, None, :, None]
    return kept.reshape(weight.shape)


def plain(tokens, gate_weight, up_weight, down_weight, gate_mask, up_mask, down_mask):
    rows = lax.all_gather(tokens, "col", axis=0, tiled=True)
    gate = jnp.dot(rows, apply_blocks(gate_weight, gate_mask), preferred_element_type=F32)
    up = jnp.dot(rows, apply_blocks(up_weight, up_mask), preferred_element_type=F32)
    gate, up = lax.psum(jnp.stack([gate, up]), "row")
    hidden = (jax.nn.silu(gate) * up).astype(BF16)
    part = jnp.dot(hidden, apply_blocks(down_weight, down_mask), preferred_element_type=F32)
    return lax.psum_scatter(part, "col", scatter_dimension=0, tiled=True).astype(BF16)


VMEM_SPEC = pl.BlockSpec(memory_space=pltpu.VMEM)
HBM_SPEC = pl.BlockSpec(memory_space=pltpu.HBM)
ANY_SPEC = pl.BlockSpec(memory_space=pl.ANY)


def in_hbm(value):
    return pltpu.with_memory_space_constraint(value, pltpu.HBM)


def in_vmem(value):
    return pltpu.with_memory_space_constraint(value, pltpu.VMEM)


def factor(mask, i, j):
    return mask[i, j].astype(F32).astype(BF16)


def loop(count, step, unroll=1):
    def body(i, carry):
        step(i)
        return carry

    lax.fori_loop(0, count, body, 0, unroll=unroll)


def cost(flops, count):
    return pl.CostEstimate(flops=flops, bytes_accessed=count, transcendentals=0)


def nothing(*refs):
    del refs


def tie(value, *deps):
    return pl.pallas_call(
        nothing,
        in_specs=[ANY_SPEC] * (1 + len(deps)),
        out_specs=ANY_SPEC,
        out_shape=jax.ShapeDtypeStruct(value.shape, value.dtype),
        input_output_aliases={0: 0},
        compiler_params=pltpu.CompilerParams(vmem_limit_bytes=MIB),
        name="tie",
    )(value, *deps)


def quarter_of(name):
    row, col = lax.axis_index("row"), lax.axis_index("col")
    step1 = 1 + lax.rem(col, 2)
    flip = {"own": 0, "second": 3 - step1, "first": step1, "last": 3}[name]
    return row ^ flip


class Pairs:
    def __init__(self, quarter, masks, weights, buf, held_masks, sem, mask_sem):
        self.quarter, self.masks, self.weights = quarter, masks, weights
        self.buf, self.held_masks, self.sem, self.mask_sem = buf, held_masks, sem, mask_sem
        self.tiles, self.depth, self.wide = buf.shape
        self.blk = self.wide // 2

    def mask_copies(self):
        return [
            pltpu.make_async_copy(m, h, self.mask_sem.at[t])
            for t, (m, h) in enumerate(zip(self.masks, self.held_masks))
        ]

    def copies(self, tile):
        column = pl.multiple_of((self.quarter * self.tiles + tile) * self.blk, self.blk)
        return [
            pltpu.make_async_copy(
                w.at[:, pl.ds(column, self.blk)],
                self.buf.at[tile, :, pl.ds(t * self.blk, self.blk)],
                self.sem.at[tile, t],
            )
            for t, w in enumerate(self.weights)
        ]

    def start(self):
        for copy in self.mask_copies():
            copy.start()

        def step(tile):
            for copy in self.copies(tile):
                copy.start()

        loop(self.tiles, step)
        for copy in self.mask_copies():
            copy.wait()

    def wait(self, tile):
        for copy in self.copies(tile):
            copy.wait()

    def masked(self, tile):
        blk = self.blk
        column = self.quarter * self.tiles + tile
        return [
            [
                self.buf[tile, a * blk : (a + 1) * blk, t * blk : (t + 1) * blk] * factor(m, a, column)
                for t, m in enumerate(self.held_masks)
            ]
            for a in range(self.depth // blk)
        ]


def pairs_scratch(mask, tiles):
    return [
        pltpu.SMEM(mask.shape, mask.dtype),
        pltpu.SMEM(mask.shape, mask.dtype),
        pltpu.SemaphoreType.DMA((tiles, 2)),
        pltpu.SemaphoreType.DMA((2,)),
    ]


def put_pair(out, tile, value):
    blk = value.shape[1] // 2
    half = out.shape[1] // 2
    for t in range(2):
        column = pl.multiple_of(t * half + tile * blk, blk)
        out[:, pl.ds(column, blk)] = value[:, t * blk : (t + 1) * blk].astype(out.dtype)


def load_pairs_kernel(name, *refs):
    buf, *held_masks, sem, mask_sem = refs[-5:]
    pairs = Pairs(quarter_of(name), refs[:2], refs[2:4], buf, held_masks, sem, mask_sem)
    blk = pairs.blk
    pairs.start()

    def keep(tile):
        pairs.wait(tile)
        for a, blocks in enumerate(pairs.masked(tile)):
            for t, value in enumerate(blocks):
                buf[tile, a * blk : (a + 1) * blk, t * blk : (t + 1) * blk] = value

    loop(pairs.tiles, keep)


def load_pairs(name, masks, weights, deps=()):
    depth, width = weights[0].shape
    blk = width // masks[0].shape[1]
    tiles = masks[0].shape[1] // 4
    return pl.pallas_call(
        functools.partial(load_pairs_kernel, name),
        in_specs=[HBM_SPEC] * 4 + [ANY_SPEC] * len(deps),
        out_specs=VMEM_SPEC,
        out_shape=pltpu.VMEM((tiles, depth, 2 * blk), BF16),
        scratch_shapes=pairs_scratch(masks[0], tiles),
        compiler_params=pltpu.CompilerParams(vmem_limit_bytes=4 * MIB),
        cost_estimate=cost(0, 2 * 2 * depth * width // 4),
        name="load_" + name,
    )(*[in_hbm(v) for v in (*masks, *weights)], *deps)


def held_pairs_kernel(count, *refs):
    x, buf, out = refs[:count], refs[count], refs[-1]

    def step(tile):
        rows = jnp.concatenate([part[...] for part in x], axis=0)
        put_pair(out, tile, jnp.dot(rows, buf[tile], preferred_element_type=F32))

    loop(buf.shape[0], step, unroll=buf.shape[0])


def held_pairs(x, buf, deps=()):
    tiles, depth, wide = buf.shape
    rows = sum(part.shape[0] for part in x)
    return pl.pallas_call(
        functools.partial(held_pairs_kernel, len(x)),
        in_specs=[VMEM_SPEC] * (len(x) + 1) + [ANY_SPEC] * len(deps),
        out_specs=VMEM_SPEC,
        out_shape=jax.ShapeDtypeStruct((rows, tiles * wide), BF16),
        compiler_params=pltpu.CompilerParams(vmem_limit_bytes=4 * MIB),
        cost_estimate=cost(2 * rows * depth * tiles * wide, 2 * tiles * depth * wide // 2),
        name="held_pairs",
    )(*[in_vmem(part) for part in x], in_vmem(buf), *deps)


def stream_pairs_kernel(name, count, rows, *refs):
    x, outs = refs[4 : 4 + count], refs[-5 - len(rows) : -5]
    buf, *held_masks, sem, mask_sem = refs[-5:]
    pairs = Pairs(quarter_of(name), refs[:2], refs[2:4], buf, held_masks, sem, mask_sem)
    pairs.start()

    def step(tile):
        pairs.wait(tile)
        w = jnp.concatenate([jnp.concatenate(row, axis=1) for row in pairs.masked(tile)], axis=0)
        value = jnp.dot(jnp.concatenate([part[...] for part in x], axis=0), w, preferred_element_type=F32)
        first = 0
        for size, out in zip(rows, outs):
            put_pair(out, tile, value[first : first + size])
            first += size

    loop(pairs.tiles, step)


def stream_pairs(name, masks, weights, groups, deps=()):
    depth, width = weights[0].shape
    blk = width // masks[0].shape[1]
    tiles = masks[0].shape[1] // 4
    x = [part for group in groups for part in group]
    rows = [sum(part.shape[0] for part in group) for group in groups]
    return pl.pallas_call(
        functools.partial(stream_pairs_kernel, name, len(x), rows),
        in_specs=[HBM_SPEC] * 4 + [VMEM_SPEC] * len(x) + [ANY_SPEC] * len(deps),
        out_specs=[VMEM_SPEC] * len(rows),
        out_shape=[jax.ShapeDtypeStruct((size, width // 2), F32) for size in rows],
        scratch_shapes=[pltpu.VMEM((tiles, depth, 2 * blk), BF16)] + pairs_scratch(masks[0], tiles),
        compiler_params=pltpu.CompilerParams(vmem_limit_bytes=22 * MIB),
        cost_estimate=cost(2 * sum(rows) * depth * width // 2, 2 * 2 * depth * width // 4),
        name="stream_" + name,
    )(*[in_hbm(v) for v in (*masks, *weights)], *[in_vmem(part) for part in x], *deps)


def load_down_kernel(names, mask_hbm, down_hbm, *refs):
    count = len(names)
    bufs, (mask, sem, mask_sem) = refs[-3 - count : -3], refs[-3:]
    panels, depth, width = bufs[0].shape
    cols = mask.shape[1]
    blk = width // cols
    first = [quarter_of(name) * panels for name in names]
    mask_copy = pltpu.make_async_copy(mask_hbm, mask, mask_sem)

    def copy(k, p):
        rows = pl.ds(pl.multiple_of((first[k] + p) * depth, depth), depth)
        return pltpu.make_async_copy(down_hbm.at[rows], bufs[k].at[p], sem.at[k, p])

    mask_copy.start()
    for k in range(count):
        loop(panels, lambda p, k=k: copy(k, p).start())
    mask_copy.wait()
    for k in range(count):

        def keep(p, k=k):
            copy(k, p).wait()
            for j in range(cols):
                at = slice(j * blk, (j + 1) * blk)
                bufs[k][p, :, at] = bufs[k][p, :, at] * factor(mask, first[k] + p, j)

        loop(panels, keep)


def load_down(names, mask, down, deps=()):
    count = len(names)
    panels = mask.shape[0] // 4
    depth, width = down.shape
    return pl.pallas_call(
        functools.partial(load_down_kernel, names),
        in_specs=[HBM_SPEC] * 2 + [ANY_SPEC] * len(deps),
        out_specs=[VMEM_SPEC] * count,
        out_shape=[pltpu.VMEM((panels, depth // mask.shape[0], width), BF16)] * count,
        scratch_shapes=[
            pltpu.SMEM(mask.shape, mask.dtype),
            pltpu.SemaphoreType.DMA((count, panels)),
            pltpu.SemaphoreType.DMA,
        ],
        compiler_params=pltpu.CompilerParams(vmem_limit_bytes=4 * MIB),
        cost_estimate=cost(0, 2 * depth * width * count // 4),
        name="load_down",
    )(in_hbm(mask), in_hbm(down), *deps)


def down_kernel(count, adds, blocks, tile, *refs):
    hidden, bufs, total = refs[:count], refs[count : 2 * count], refs[2 * count]
    outs, rows = refs[-1 - blocks : -1], refs[-1]
    panels, blk, width = bufs[0].shape
    depth = panels * blk
    for k, part in enumerate(hidden):
        rows[:, k * depth : (k + 1) * depth] = part[...]

    def step(n):
        at = pl.ds(pl.multiple_of(n * tile, tile), tile)
        w = jnp.concatenate([buf[:, :, at].reshape(depth, tile) for buf in bufs], axis=0)
        value = jnp.dot(rows[...], w, preferred_element_type=F32)
        if adds:
            value = value + total[:, at]
        size = value.shape[0] // blocks
        for k, out in enumerate(outs):
            out[:, at] = value[k * size : (k + 1) * size]

    loop(width // tile, step, unroll=width // tile)


def down(hidden, bufs, total=(), blocks=1, tile=512, deps=()):
    panels, blk, width = bufs[0].shape
    rows, depth, count = hidden[0].shape[0], len(hidden) * panels * blk, len(hidden)
    return pl.pallas_call(
        functools.partial(down_kernel, count, len(total), blocks, tile),
        in_specs=[VMEM_SPEC] * (2 * count + len(total)) + [ANY_SPEC] * len(deps),
        out_specs=[VMEM_SPEC] * blocks,
        out_shape=[jax.ShapeDtypeStruct((rows // blocks, width), F32)] * blocks,
        scratch_shapes=[pltpu.VMEM((rows, depth), BF16)],
        compiler_params=pltpu.CompilerParams(vmem_limit_bytes=4 * MIB),
        cost_estimate=cost(2 * rows * depth * width, 2 * depth * width),
        name="down",
    )(*[in_vmem(v) for v in (*hidden, *bufs, *total)], *deps)


def added_kernel(count, *refs):
    base, parts, out = refs[0], refs[1 : 1 + count], refs[-1]
    first = 0
    for part in parts:
        at = slice(first, first + part.shape[0])
        out[at] = (base[at] + part[...].astype(F32)).astype(out.dtype)
        first += part.shape[0]


def added(base, parts, deps=()):
    return pl.pallas_call(
        functools.partial(added_kernel, len(parts)),
        in_specs=[VMEM_SPEC] * (1 + len(parts)) + [ANY_SPEC] * len(deps),
        out_specs=VMEM_SPEC,
        out_shape=jax.ShapeDtypeStruct(base.shape, BF16),
        compiler_params=pltpu.CompilerParams(vmem_limit_bytes=4 * MIB),
        cost_estimate=cost(0, 8 * base.size),
        name="added",
    )(*[in_vmem(v) for v in (base, *parts)], *deps)


def gated_kernel(first, own, got_first, got_second, *refs):
    out = refs[-1]
    rows, width = out.shape
    gate, up = [
        own[:, at] + got_first[:, at].astype(F32) + got_second[first : first + rows, at].astype(F32)
        for at in (slice(0, width), slice(width, 2 * width))
    ]
    out[...] = (jax.nn.silu(gate) * up).astype(out.dtype)


def gated(own, got_first, got_second, first, deps=()):
    rows, width = own.shape
    return pl.pallas_call(
        functools.partial(gated_kernel, first),
        in_specs=[VMEM_SPEC] * 3 + [ANY_SPEC] * len(deps),
        out_specs=VMEM_SPEC,
        out_shape=jax.ShapeDtypeStruct((rows, width // 2), BF16),
        compiler_params=pltpu.CompilerParams(vmem_limit_bytes=8 * MIB),
        cost_estimate=cost(0, 8 * rows * width),
        name="gated",
    )(in_vmem(own), in_vmem(got_first), in_vmem(got_second), *deps)


class Exchange:
    def __init__(self, rows, cols):
        self.rows, self.cols = rows, cols

    def swap(self, value, row_bits, col_bits):
        pairs = []
        for r in range(self.rows):
            for c in range(self.cols):
                pairs.append((r * self.cols + c, (r ^ row_bits(c)) * self.cols + (c ^ col_bits)))
        return lax.ppermute(value, ("row", "col"), pairs)

    def core(self, value):
        return self.swap(value, lambda c: 0, 1)

    def near(self, value):
        return self.swap(value, lambda c: 0, 2)

    def far(self, value):
        return self.swap(value, lambda c: 0, 4)

    def diagonal(self, value):
        return self.swap(value, lambda c: 0, 6)

    def first(self, value):
        return self.swap(value, lambda c: 1 + (c & 1), 0)

    def second(self, value):
        return self.swap(value, lambda c: 2 - (c & 1), 0)


def paired(tokens, gate_weight, up_weight, down_weight, gate_mask, up_mask, down_mask, swap):
    weights = (gate_weight, up_weight)
    masks = (gate_mask, up_mask)
    width = gate_weight.shape[1] // 4
    blk = tokens.shape[0]

    near = swap.near(tokens)
    far = swap.far(tokens)
    core = swap.core(tokens)
    w_last = load_pairs("last", masks, weights)
    w_first = load_pairs("first", masks, weights, deps=(w_last,))
    near = tie(near, w_first)
    far = tie(far, w_first)
    far_near = swap.near(far)
    close = (tokens, near, core, swap.core(near))
    close_last = held_pairs(close, w_last)
    got_close_last = swap.first(close_last)
    close_first = held_pairs(close, w_first, deps=(close_last,))
    got_close_first = swap.first(close_first)
    far_near = tie(far_near, close_first)
    distant = (far, far_near, swap.core(far), swap.core(far_near))
    distant_last = tie(held_pairs(distant, w_last), got_close_last)
    got_distant_last = swap.first(distant_last)
    (second,) = stream_pairs(
        "second", masks, weights, (distant + close,), deps=(distant_last, close_first)
    )
    second = added(second, (got_distant_last, got_close_last), deps=(got_close_first,))
    got_second = swap.second(second)
    distant_first = held_pairs(distant, w_first, deps=(second,))
    got_distant_first = swap.first(distant_first)
    distant_own, close_own = stream_pairs("own", masks, weights, (distant, close), deps=(distant_first,))

    source = (down_mask, down_weight)
    down_own, down_second = load_down(("own", "second"), *source, deps=(distant_own,))
    distant = gated(distant_own, got_distant_first, got_second, 0, deps=(down_own,))
    close = gated(close_own, got_close_first, got_second, 4 * blk, deps=(distant,))
    second, first = swap.second(distant), swap.first(distant)
    down_first, down_last = load_down(("first", "last"), *source, deps=(close,))
    second = tie(second, down_last)
    last = swap.first(second)
    close = tie(close, second)
    close_second, close_first = swap.second(close), swap.first(close)
    total = down((distant, second, first), (down_own, down_second, down_first))
    mine, other = down((last,), (down_last,), total, blocks=2)
    other = tie(other, close_second, close_first)

    mine = mine + swap.core(other)
    total = down((close,), (down_own,), deps=(other,))
    close_second = tie(close_second, *total)
    close_last = swap.first(close_second)
    near_rows, far_rows = mine[blk:].astype(BF16), mine[:blk]
    got_near = swap.near(near_rows)
    total = down((close_second, close_first), (down_second, down_first), total, deps=(near_rows,))
    far_rows = (far_rows + got_near).astype(BF16)
    got_far = swap.far(far_rows)
    mine, other = down((close_last,), (down_last,), total, blocks=2)
    mine = mine + swap.core(tie(other, far_rows))
    return (mine[:blk] + swap.near(mine[blk:].astype(BF16)) + got_far).astype(BF16)


def solution(mesh):
    rows, cols = mesh.shape["row"], mesh.shape["col"]
    body = plain
    if (rows, cols) == (4, 8):
        body = functools.partial(paired, swap=Exchange(rows, cols))
    return jax.shard_map(
        body,
        mesh=mesh,
        in_specs=(
            P("col", "row"),
            P("row", "col"),
            P("row", "col"),
            P("col", "row"),
            P("row", "col"),
            P("row", "col"),
            P("col", "row"),
        ),
        out_specs=P("col", "row"),
        check_vma=False,
    )
```

```python
import functools

import jax
import jax.numpy as jnp
from jax import lax
from jax.experimental import pallas as pl
from jax.experimental.pallas import tpu as pltpu
from jax.sharding import PartitionSpec as P

BF16 = jnp.bfloat16
F32 = jnp.float32
MIB = 1 << 20


def apply_blocks(weight, mask):
    block_rows, block_cols = mask.shape
    shaped = weight.reshape(
        block_rows, weight.shape[0] // block_rows, block_cols, weight.shape[1] // block_cols
    )
    kept = shaped * mask.astype(weight.dtype)[:, None, :, None]
    return kept.reshape(weight.shape)


def plain(tokens, gate_weight, up_weight, down_weight, gate_mask, up_mask, down_mask):
    rows = lax.all_gather(tokens, "col", axis=0, tiled=True)
    gate = jnp.dot(rows, apply_blocks(gate_weight, gate_mask), preferred_element_type=F32)
    up = jnp.dot(rows, apply_blocks(up_weight, up_mask), preferred_element_type=F32)
    gate, up = lax.psum(jnp.stack([gate, up]), "row")
    hidden = (jax.nn.silu(gate) * up).astype(BF16)
    part = jnp.dot(hidden, apply_blocks(down_weight, down_mask), preferred_element_type=F32)
    return lax.psum_scatter(part, "col", scatter_dimension=0, tiled=True).astype(BF16)


VMEM_SPEC = pl.BlockSpec(memory_space=pltpu.VMEM)
HBM_SPEC = pl.BlockSpec(memory_space=pltpu.HBM)
ANY_SPEC = pl.BlockSpec(memory_space=pl.ANY)


def in_hbm(value):
    return pltpu.with_memory_space_constraint(value, pltpu.HBM)


def in_vmem(value):
    return pltpu.with_memory_space_constraint(value, pltpu.VMEM)


def factor(mask, i, j):
    return mask[i, j].astype(F32).astype(BF16)


def loop(count, step, unroll=1):
    def body(i, carry):
        step(i)
        return carry

    lax.fori_loop(0, count, body, 0, unroll=unroll)


def cost(flops, count):
    return pl.CostEstimate(flops=flops, bytes_accessed=count, transcendentals=0)


def nothing(*refs):
    del refs


def tie(value, *deps):
    return pl.pallas_call(
        nothing,
        in_specs=[ANY_SPEC] * (1 + len(deps)),
        out_specs=ANY_SPEC,
        out_shape=jax.ShapeDtypeStruct(value.shape, value.dtype),
        input_output_aliases={0: 0},
        compiler_params=pltpu.CompilerParams(vmem_limit_bytes=MIB),
        name="tie",
    )(value, *deps)


def quarter_of(name):
    row, col = lax.axis_index("row"), lax.axis_index("col")
    step1 = 1 + lax.rem(col, 2)
    flip = {"own": 0, "second": 3 - step1, "first": step1, "last": 3}[name]
    return row ^ flip


class Pairs:
    def __init__(self, quarter, masks, weights, buf, held_masks, sem, mask_sem):
        self.quarter, self.masks, self.weights = quarter, masks, weights
        self.buf, self.held_masks, self.sem, self.mask_sem = buf, held_masks, sem, mask_sem
        self.tiles, self.depth, self.wide = buf.shape
        self.blk = self.wide // 2

    def mask_copies(self):
        return [
            pltpu.make_async_copy(m, h, self.mask_sem.at[t])
            for t, (m, h) in enumerate(zip(self.masks, self.held_masks))
        ]

    def copies(self, tile):
        column = pl.multiple_of((self.quarter * self.tiles + tile) * self.blk, self.blk)
        return [
            pltpu.make_async_copy(
                w.at[:, pl.ds(column, self.blk)],
                self.buf.at[tile, :, pl.ds(t * self.blk, self.blk)],
                self.sem.at[tile, t],
            )
            for t, w in enumerate(self.weights)
        ]

    def start(self):
        for copy in self.mask_copies():
            copy.start()

        def step(tile):
            for copy in self.copies(tile):
                copy.start()

        loop(self.tiles, step)
        for copy in self.mask_copies():
            copy.wait()

    def wait(self, tile):
        for copy in self.copies(tile):
            copy.wait()

    def masked(self, tile):
        blk = self.blk
        column = self.quarter * self.tiles + tile
        return [
            [
                self.buf[tile, a * blk : (a + 1) * blk, t * blk : (t + 1) * blk] * factor(m, a, column)
                for t, m in enumerate(self.held_masks)
            ]
            for a in range(self.depth // blk)
        ]


def pairs_scratch(mask, tiles):
    return [
        pltpu.SMEM(mask.shape, mask.dtype),
        pltpu.SMEM(mask.shape, mask.dtype),
        pltpu.SemaphoreType.DMA((tiles, 2)),
        pltpu.SemaphoreType.DMA((2,)),
    ]


def put_pair(out, tile, value):
    blk = value.shape[1] // 2
    half = out.shape[1] // 2
    for t in range(2):
        column = pl.multiple_of(t * half + tile * blk, blk)
        out[:, pl.ds(column, blk)] = value[:, t * blk : (t + 1) * blk].astype(out.dtype)


def load_pairs_kernel(name, *refs):
    buf, *held_masks, sem, mask_sem = refs[-5:]
    pairs = Pairs(quarter_of(name), refs[:2], refs[2:4], buf, held_masks, sem, mask_sem)
    blk = pairs.blk
    pairs.start()

    def keep(tile):
        pairs.wait(tile)
        for a, blocks in enumerate(pairs.masked(tile)):
            for t, value in enumerate(blocks):
                buf[tile, a * blk : (a + 1) * blk, t * blk : (t + 1) * blk] = value

    loop(pairs.tiles, keep)


def load_pairs(name, masks, weights, deps=()):
    depth, width = weights[0].shape
    blk = width // masks[0].shape[1]
    tiles = masks[0].shape[1] // 4
    return pl.pallas_call(
        functools.partial(load_pairs_kernel, name),
        in_specs=[HBM_SPEC] * 4 + [ANY_SPEC] * len(deps),
        out_specs=VMEM_SPEC,
        out_shape=pltpu.VMEM((tiles, depth, 2 * blk), BF16),
        scratch_shapes=pairs_scratch(masks[0], tiles),
        compiler_params=pltpu.CompilerParams(vmem_limit_bytes=4 * MIB),
        cost_estimate=cost(0, 2 * 2 * depth * width // 4),
        name="load_" + name,
    )(*[in_hbm(v) for v in (*masks, *weights)], *deps)


def held_pairs_kernel(count, *refs):
    x, buf, out = refs[:count], refs[count], refs[-1]

    def step(tile):
        rows = jnp.concatenate([part[...] for part in x], axis=0)
        put_pair(out, tile, jnp.dot(rows, buf[tile], preferred_element_type=F32))

    loop(buf.shape[0], step, unroll=buf.shape[0])


def held_pairs(x, buf, deps=()):
    tiles, depth, wide = buf.shape
    rows = sum(part.shape[0] for part in x)
    return pl.pallas_call(
        functools.partial(held_pairs_kernel, len(x)),
        in_specs=[VMEM_SPEC] * (len(x) + 1) + [ANY_SPEC] * len(deps),
        out_specs=VMEM_SPEC,
        out_shape=jax.ShapeDtypeStruct((rows, tiles * wide), BF16),
        compiler_params=pltpu.CompilerParams(vmem_limit_bytes=4 * MIB),
        cost_estimate=cost(2 * rows * depth * tiles * wide, 2 * tiles * depth * wide // 2),
        name="held_pairs",
    )(*[in_vmem(part) for part in x], in_vmem(buf), *deps)


def stream_pairs_kernel(name, count, rows, *refs):
    x, outs = refs[4 : 4 + count], refs[-5 - len(rows) : -5]
    buf, *held_masks, sem, mask_sem = refs[-5:]
    pairs = Pairs(quarter_of(name), refs[:2], refs[2:4], buf, held_masks, sem, mask_sem)
    pairs.start()

    def step(tile):
        pairs.wait(tile)
        w = jnp.concatenate([jnp.concatenate(row, axis=1) for row in pairs.masked(tile)], axis=0)
        value = jnp.dot(jnp.concatenate([part[...] for part in x], axis=0), w, preferred_element_type=F32)
        first = 0
        for size, out in zip(rows, outs):
            put_pair(out, tile, value[first : first + size])
            first += size

    loop(pairs.tiles, step)


def stream_pairs(name, masks, weights, groups, deps=()):
    depth, width = weights[0].shape
    blk = width // masks[0].shape[1]
    tiles = masks[0].shape[1] // 4
    x = [part for group in groups for part in group]
    rows = [sum(part.shape[0] for part in group) for group in groups]
    return pl.pallas_call(
        functools.partial(stream_pairs_kernel, name, len(x), rows),
        in_specs=[HBM_SPEC] * 4 + [VMEM_SPEC] * len(x) + [ANY_SPEC] * len(deps),
        out_specs=[VMEM_SPEC] * len(rows),
        out_shape=[jax.ShapeDtypeStruct((size, width // 2), F32) for size in rows],
        scratch_shapes=[pltpu.VMEM((tiles, depth, 2 * blk), BF16)] + pairs_scratch(masks[0], tiles),
        compiler_params=pltpu.CompilerParams(vmem_limit_bytes=22 * MIB),
        cost_estimate=cost(2 * sum(rows) * depth * width // 2, 2 * 2 * depth * width // 4),
        name="stream_" + name,
    )(*[in_hbm(v) for v in (*masks, *weights)], *[in_vmem(part) for part in x], *deps)


def load_down_kernel(names, mask_hbm, down_hbm, *refs):
    count = len(names)
    bufs, (mask, sem, mask_sem) = refs[-3 - count : -3], refs[-3:]
    panels, depth, width = bufs[0].shape
    cols = mask.shape[1]
    blk = width // cols
    first = [quarter_of(name) * panels for name in names]
    mask_copy = pltpu.make_async_copy(mask_hbm, mask, mask_sem)

    def copy(k, p):
        rows = pl.ds(pl.multiple_of((first[k] + p) * depth, depth), depth)
        return pltpu.make_async_copy(down_hbm.at[rows], bufs[k].at[p], sem.at[k, p])

    mask_copy.start()
    for k in range(count):
        loop(panels, lambda p, k=k: copy(k, p).start())
    mask_copy.wait()
    for k in range(count):

        def keep(p, k=k):
            copy(k, p).wait()
            for j in range(cols):
                at = slice(j * blk, (j + 1) * blk)
                bufs[k][p, :, at] = bufs[k][p, :, at] * factor(mask, first[k] + p, j)

        loop(panels, keep)


def load_down(names, mask, down, deps=()):
    count = len(names)
    panels = mask.shape[0] // 4
    depth, width = down.shape
    return pl.pallas_call(
        functools.partial(load_down_kernel, names),
        in_specs=[HBM_SPEC] * 2 + [ANY_SPEC] * len(deps),
        out_specs=[VMEM_SPEC] * count,
        out_shape=[pltpu.VMEM((panels, depth // mask.shape[0], width), BF16)] * count,
        scratch_shapes=[
            pltpu.SMEM(mask.shape, mask.dtype),
            pltpu.SemaphoreType.DMA((count, panels)),
            pltpu.SemaphoreType.DMA,
        ],
        compiler_params=pltpu.CompilerParams(vmem_limit_bytes=4 * MIB),
        cost_estimate=cost(0, 2 * depth * width * count // 4),
        name="load_down",
    )(in_hbm(mask), in_hbm(down), *deps)


def down_kernel(count, adds, blocks, tile, *refs):
    hidden, bufs, total = refs[:count], refs[count : 2 * count], refs[2 * count]
    outs, rows = refs[-1 - blocks : -1], refs[-1]
    panels, blk, width = bufs[0].shape
    depth = panels * blk
    for k, part in enumerate(hidden):
        rows[:, k * depth : (k + 1) * depth] = part[...]

    def step(n):
        at = pl.ds(pl.multiple_of(n * tile, tile), tile)
        w = jnp.concatenate([buf[:, :, at].reshape(depth, tile) for buf in bufs], axis=0)
        value = jnp.dot(rows[...], w, preferred_element_type=F32)
        if adds:
            value = value + total[:, at]
        size = value.shape[0] // blocks
        for k, out in enumerate(outs):
            out[:, at] = value[k * size : (k + 1) * size]

    loop(width // tile, step, unroll=width // tile)


def down(hidden, bufs, total=(), blocks=1, tile=512, deps=()):
    panels, blk, width = bufs[0].shape
    rows, depth, count = hidden[0].shape[0], len(hidden) * panels * blk, len(hidden)
    return pl.pallas_call(
        functools.partial(down_kernel, count, len(total), blocks, tile),
        in_specs=[VMEM_SPEC] * (2 * count + len(total)) + [ANY_SPEC] * len(deps),
        out_specs=[VMEM_SPEC] * blocks,
        out_shape=[jax.ShapeDtypeStruct((rows // blocks, width), F32)] * blocks,
        scratch_shapes=[pltpu.VMEM((rows, depth), BF16)],
        compiler_params=pltpu.CompilerParams(vmem_limit_bytes=4 * MIB),
        cost_estimate=cost(2 * rows * depth * width, 2 * depth * width),
        name="down",
    )(*[in_vmem(v) for v in (*hidden, *bufs, *total)], *deps)


def added_kernel(count, *refs):
    base, parts, out = refs[0], refs[1 : 1 + count], refs[-1]
    first = 0
    for part in parts:
        at = slice(first, first + part.shape[0])
        out[at] = (base[at] + part[...].astype(F32)).astype(out.dtype)
        first += part.shape[0]


def added(base, parts, deps=()):
    return pl.pallas_call(
        functools.partial(added_kernel, len(parts)),
        in_specs=[VMEM_SPEC] * (1 + len(parts)) + [ANY_SPEC] * len(deps),
        out_specs=VMEM_SPEC,
        out_shape=jax.ShapeDtypeStruct(base.shape, BF16),
        compiler_params=pltpu.CompilerParams(vmem_limit_bytes=4 * MIB),
        cost_estimate=cost(0, 8 * base.size),
        name="added",
    )(*[in_vmem(v) for v in (base, *parts)], *deps)


def gated_kernel(first, own, got_first, got_second, *refs):
    out = refs[-1]
    rows, width = out.shape
    gate, up = [
        own[:, at] + got_first[:, at].astype(F32) + got_second[first : first + rows, at].astype(F32)
        for at in (slice(0, width), slice(width, 2 * width))
    ]
    out[...] = (jax.nn.silu(gate) * up).astype(out.dtype)


def gated(own, got_first, got_second, first, deps=()):
    rows, width = own.shape
    return pl.pallas_call(
        functools.partial(gated_kernel, first),
        in_specs=[VMEM_SPEC] * 3 + [ANY_SPEC] * len(deps),
        out_specs=VMEM_SPEC,
        out_shape=jax.ShapeDtypeStruct((rows, width // 2), BF16),
        compiler_params=pltpu.CompilerParams(vmem_limit_bytes=8 * MIB),
        cost_estimate=cost(0, 8 * rows * width),
        name="gated",
    )(in_vmem(own), in_vmem(got_first), in_vmem(got_second), *deps)


class Exchange:
    def __init__(self, rows, cols):
        self.rows, self.cols = rows, cols

    def swap(self, value, row_bits, col_bits):
        pairs = []
        for r in range(self.rows):
            for c in range(self.cols):
                pairs.append((r * self.cols + c, (r ^ row_bits(c)) * self.cols + (c ^ col_bits)))
        return lax.ppermute(value, ("row", "col"), pairs)

    def core(self, value):
        return self.swap(value, lambda c: 0, 1)

    def near(self, value):
        return self.swap(value, lambda c: 0, 2)

    def far(self, value):
        return self.swap(value, lambda c: 0, 4)

    def diagonal(self, value):
        return self.swap(value, lambda c: 0, 6)

    def first(self, value):
        return self.swap(value, lambda c: 1 + (c & 1), 0)

    def second(self, value):
        return self.swap(value, lambda c: 2 - (c & 1), 0)


def paired(tokens, gate_weight, up_weight, down_weight, gate_mask, up_mask, down_mask, swap):
    weights = (gate_weight, up_weight)
    masks = (gate_mask, up_mask)
    width = gate_weight.shape[1] // 4
    blk = tokens.shape[0]

    near = swap.near(tokens)
    far = swap.far(tokens)
    core = swap.core(tokens)
    w_last = load_pairs("last", masks, weights)
    w_first = load_pairs("first", masks, weights, deps=(w_last,))
    near = tie(near, w_first)
    far = tie(far, w_first)
    far_near = swap.near(far)
    close = (tokens, near, core, swap.core(near))
    close_last = held_pairs(close, w_last)
    got_close_last = swap.first(close_last)
    close_first = held_pairs(close, w_first, deps=(close_last,))
    got_close_first = swap.first(close_first)
    far_near = tie(far_near, close_first)
    distant = (far, far_near, swap.core(far), swap.core(far_near))
    distant_last = tie(held_pairs(distant, w_last), got_close_last)
    got_distant_last = swap.first(distant_last)
    (second,) = stream_pairs(
        "second", masks, weights, (distant + close,), deps=(distant_last, close_first)
    )
    second = added(second, (got_distant_last, got_close_last), deps=(got_close_first,))
    got_second = swap.second(second)
    distant_first = held_pairs(distant, w_first, deps=(second,))
    got_distant_first = swap.first(distant_first)
    distant_own, close_own = stream_pairs("own", masks, weights, (distant, close), deps=(distant_first,))

    source = (down_mask, down_weight)
    down_own, down_second = load_down(("own", "second"), *source, deps=(distant_own,))
    distant = gated(distant_own, got_distant_first, got_second, 0, deps=(down_own,))
    close = gated(close_own, got_close_first, got_second, 4 * blk, deps=(distant,))
    second, first = swap.second(distant), swap.first(distant)
    down_first, down_last = load_down(("first", "last"), *source, deps=(close,))
    second = tie(second, down_last)
    last = swap.first(second)
    close_second, close_first = swap.second(close), swap.first(close)
    total = down((distant, second, first), (down_own, down_second, down_first))
    mine, other = down((last,), (down_last,), total, blocks=2)
    other = tie(other, close_second, close_first)

    mine = mine + swap.core(other)
    total = down((close,), (down_own,), deps=(other,))
    close_second = tie(close_second, *total)
    close_last = swap.first(close_second)
    near_rows, far_rows = mine[blk:].astype(BF16), mine[:blk]
    got_near = swap.near(near_rows)
    total = down((close_second, close_first), (down_second, down_first), total, deps=(near_rows,))
    far_rows = (far_rows + got_near).astype(BF16)
    got_far = swap.far(far_rows)
    mine, other = down((close_last,), (down_last,), total, blocks=2)
    mine = mine + swap.core(tie(other, far_rows))
    return (mine[:blk] + swap.near(mine[blk:].astype(BF16)) + got_far).astype(BF16)


def solution(mesh):
    rows, cols = mesh.shape["row"], mesh.shape["col"]
    body = plain
    if (rows, cols) == (4, 8):
        body = functools.partial(paired, swap=Exchange(rows, cols))
    return jax.shard_map(
        body,
        mesh=mesh,
        in_specs=(
            P("col", "row"),
            P("row", "col"),
            P("row", "col"),
            P("col", "row"),
            P("row", "col"),
            P("row", "col"),
            P("col", "row"),
        ),
        out_specs=P("col", "row"),
        check_vma=False,
    )
```
